32 devices in a mesh: season: 4 (over y, x), strip: 8 (over z, core).
Axes of the slice: x: 2, y: 2, z: 4, core: 2. Of those that a mesh axis runs over, the one named last changes fastest.
Arguments:
- noise: float32 [32, 128, 1280], P('season', 'strip'), parts along dimension 0, may hold values from -6 to 6
- kern_row: float32 [31], replicated, may hold values from 0.05 to 0.3
- kern_col: float32 [31], replicated, may hold values from 0.05 to 0.3
- base_yield: float32 [16, 128, 1280], P(None, 'strip'), may hold values from 1 to 4
- sensitivity: float32 [16], replicated, may hold values from 0.1 to 0.5
- crop_mask: int32 [16, 128, 1280], P(None, 'strip'), may hold values 0 or 1
- cell_area: float32 [128, 1280], P('strip'), may hold values from 0.2 to 1
- cell_unit: int32 [128, 1280], P('strip'), may hold values from 0 to 815, as said below
- guarantee: float32 [16], replicated, may hold values from 1.5 to 3
- insured: float32 [16], replicated, may hold values from 0.5 to 2
Outputs:
- payout: float32 [32, 128, 1280], P('season', 'strip'), parts along dimension 0
- unit_yield: float32 [32, 16, 816], P('season', None, 'strip'), parts along dimension 0
The draws below stay inside these ranges and needn't reach their ends.
There are 4 independent parts, one for each index of `season`. The reference program is written for one: setup_inputs(seed, part) draws one part's arguments, and reference() takes and returns one part's arrays. A program takes and returns all parts, laid end to end along the dimension named above; an argument that names none is the same for every part. Nothing has to cross between parts.
Inputs may be any that keep to these rules, and one draw needn't show every extreme that they name: `cell_unit`: a cell in grid row r belongs to a unit from 102 * (r // 16 - 1) to 102 * (r // 16 + 2) - 1.
All inputs are finite; a program needn't handle non-finite values. No bound on the sum of `crop_mask` on one device may be relied on, other than what follows from the above.
Results may differ from the reference program's by a relative error of at most 0.0058.
Values may be sent and summed in bfloat16 or wider, within the bound.
A program may use at most 128 MiB of HBM per device.

```python
import math
import jax
import jax.numpy as jnp
from jax import lax

SEAS = 8
CROPS = 16
ROWS_DEV = 16
COLS = 1280
TAPS = 31
UNIT_DEV = 102
NROWS = 128
UNITS = 816


def draw_cell_unit(key, part):
    key = jax.random.fold_in(key, 11)
    first, second = jax.random.split(key)
    rows = jnp.arange(NROWS, dtype=jnp.int32)[:, None]
    cols = jnp.arange(COLS, dtype=jnp.int32)[None, :]
    strips = NROWS // ROWS_DEV
    home = rows // ROWS_DEV
    local_row = rows % ROWS_DEV
    band = cols * UNIT_DEV // COLS
    jitter = jax.random.randint(first, (NROWS, COLS), -1, 2)
    inner = ((cols > 0) & (cols < COLS - 1)).astype(jnp.int32)
    band = jnp.clip(band + jitter * inner, 0, UNIT_DEV - 1)
    coin = jax.random.randint(second, (NROWS, COLS), 0, 2)
    lower = ((local_row < 3) & (coin == 1) & (home > 0)).astype(jnp.int32)
    upper = ((local_row >= ROWS_DEV - 3) & (coin == 1) & (home < strips - 1)).astype(jnp.int32)
    owner = home - lower + upper
    return (owner * UNIT_DEV + band).astype(jnp.int32)


def touch_ends(drawn, own_key, smallest, high):
    place = [jax.random.randint(jax.random.fold_in(own_key, axis), (), 0, length) for axis, length in enumerate(drawn.shape)]
    widest = drawn.shape.index(max(drawn.shape))
    neighbour = place[:widest] + [(place[widest] + 1) % drawn.shape[widest]] + place[widest + 1:]
    return drawn.at[tuple(place)].set(smallest).at[tuple(neighbour)].set(high)


def levels(stream_key, shape, cuts, low, top_value):
    loudness = 1.0
    for axis_at, parts in cuts:
        draws = jax.random.uniform(jax.random.fold_in(jax.random.fold_in(stream_key, 6), axis_at), (parts,), jnp.float32, low / len(cuts), top_value / len(cuts))
        loudness = loudness * jnp.repeat(jnp.exp(draws), shape[axis_at] // parts).reshape((-1,) + (1,) * (len(shape) - 1 - axis_at))
    return loudness


def gaussian(stream_key, dims, width, most, pieces=(), kind=jnp.bfloat16):
    array = jax.random.normal(stream_key, dims, jnp.float32) * width
    if len(pieces) > 0:
        array = levels(stream_key, dims, pieces, -0.22, 0.18) * array
    return jnp.clip(array, min=-most, max=most).astype(kind)


def setup_inputs(seed: int = 0, part: int = 0) -> dict:
    seeds = jax.random.split(jax.random.key(seed), 11)
    part_keys = jax.random.split(jax.random.fold_in(seeds[10], part), 11)
    return {
        "noise": gaussian(part_keys[0], (SEAS, NROWS, COLS), 1.0, 6.0, ((1, 8),), jnp.float32),
        "kern_row": jnp.clip(jax.random.uniform(seeds[1], (TAPS,), jnp.float32, 0.05, 0.3), 0.05, 0.3),
        "kern_col": jnp.clip(jax.random.uniform(seeds[2], (TAPS,), jnp.float32, 0.05, 0.3), 0.05, 0.3),
        "base_yield": jnp.clip(jnp.exp(math.log(4.0) - 1.3862944 * jax.random.uniform(seeds[3], (CROPS, NROWS, COLS), jnp.float32) ** levels(seeds[3], (CROPS, NROWS, COLS), ((1, 8),), -0.2, 0.2)), 1.0, 4.0),
        "sensitivity": jnp.clip(jax.random.uniform(seeds[4], (CROPS,), jnp.float32, 0.1, 0.5), 0.1, 0.5),
        "crop_mask": touch_ends((jax.random.randint(seeds[5], (CROPS, NROWS, COLS), 0, 32) < 1).astype(jnp.int32), jax.random.fold_in(seeds[5], 1), 0, 1),
        "cell_area": jnp.clip(0.2 + 0.8 * jax.random.uniform(seeds[6], (NROWS, COLS), jnp.float32) ** levels(seeds[6], (NROWS, COLS), ((0, 8),), -0.2, 0.2), 0.2, 1.0),
        "cell_unit": draw_cell_unit(jax.random.fold_in(seeds[10], 71), part),
        "guarantee": jnp.clip(jax.random.uniform(seeds[8], (CROPS,), jnp.float32, 1.5, 3.0), 1.5, 3.0),
        "insured": jnp.clip(jnp.exp(jax.random.uniform(seeds[9], (CROPS,), jnp.float32, math.log(0.5), math.log(2.0))), 0.5, 2.0),
    }


def smooth(noise, kern_row, kern_col):
    reach = (TAPS - 1) // 2
    padded = jnp.pad(noise, ((0, 0), (reach, reach), (reach, reach)))
    across = jnp.zeros((noise.shape[0], NROWS + 2 * reach, COLS), jnp.float32)
    for j in range(TAPS):
        across = across + kern_col[j] * padded[:, :, j:j + COLS]
    field = jnp.zeros(noise.shape, jnp.float32)
    for i in range(TAPS):
        field = field + kern_row[i] * across[:, i:i + NROWS, :]
    return field


def reference(noise, kern_row, kern_col, base_yield, sensitivity, crop_mask, cell_area, cell_unit, guarantee, insured):
    field = smooth(noise, kern_row, kern_col)
    weight = (crop_mask.astype(jnp.float32) * cell_area[None]).astype(jnp.bfloat16)
    flat_unit = cell_unit.reshape(-1).astype(jnp.int32)
    weight_flat = weight.reshape(CROPS, -1).astype(jnp.float32)
    unit_area = jax.ops.segment_sum(weight_flat.T, flat_unit, UNITS)
    denom = jnp.maximum(unit_area, 1.0)

    def per_season(season_field):
        yields = base_yield * jnp.exp(sensitivity[:, None, None] * season_field[None])
        value = (weight.astype(jnp.float32) * yields).astype(jnp.bfloat16)
        sums = jax.ops.segment_sum(value.reshape(CROPS, -1).astype(jnp.float32).T, flat_unit, UNITS)
        yields_unit = sums / denom
        short = (jnp.maximum(guarantee[None] - yields_unit, 0.0) / guarantee[None]).astype(jnp.bfloat16)
        cell_short = short.astype(jnp.float32)[flat_unit]
        pay = jnp.sum(weight_flat.T * insured[None] * cell_short, axis=1)
        return pay.reshape(NROWS, COLS), yields_unit.T

    payout, unit_yield = lax.map(per_season, field)
    return payout, unit_yield
```

```python
import functools

import jax
import jax.numpy as jnp
from jax import lax
from jax.experimental import pallas as pl
from jax.experimental.pallas import tpu as pltpu
from jax.sharding import PartitionSpec as P

UNIT_DEV = 102
SPAN = 112
WIDE = 256
LOG2E = 1.4426950408889634
MESH = pl.DeviceIdType.MESH
F32 = jnp.float32
BF16 = jnp.bfloat16


def dot(a, b):
    return jnp.dot(a, b, preferred_element_type=F32)


def split(x):
    high = x.astype(BF16)
    return high, (x - high.astype(F32)).astype(BF16)


def kernel(
    n,
    noise_hbm,
    kern_row,
    kern_col,
    base_hbm,
    sens,
    mask_hbm,
    area_hbm,
    unit_hbm,
    guar,
    ins,
    pay_out,
    yield_out,
    noise,
    base,
    mask,
    area,
    unit,
    halo_lo,
    halo_hi,
    row_hi,
    row_lo,
    col_hi,
    col_lo,
    smooth_hi,
    smooth_lo,
    field,
    onehot,
    wins,
    wbase,
    wts,
    value,
    part,
    from_lo,
    from_hi,
    short,
    short_lo,
    short_hi,
    turned,
    window,
    pay,
    local_sem,
    halo_send,
    halo_recv,
    part_send,
    part_recv,
    short_send,
    short_recv,
):
    seasons, rows, cols = noise.shape
    crops = base.shape[0] // rows
    taps = kern_row.shape[0]
    reach = (taps - 1) // 2
    many = seasons * crops
    chunks = cols // WIDE
    cells = rows * WIDE
    me = lax.axis_index("strip")
    has_lo, has_hi = me > 0, me < n - 1

    def copies(source, target, sem):
        copy = pltpu.make_async_copy(source, target, local_sem.at[sem])
        copy.start()
        return copy

    get_unit = copies(unit_hbm, unit, 0)
    get_area = copies(area_hbm, area, 1)
    get_mask = copies(mask_hbm, mask, 2)
    get_base = copies(base_hbm, base, 3)
    get_noise = copies(noise_hbm, noise, 4)

    barrier = pltpu.get_barrier_semaphore()

    def each_side(body):
        @pl.when(has_lo)
        def _():
            body(0, me - 1)

        @pl.when(has_hi)
        def _():
            body(1, me + 1)

    each_side(
        lambda side, peer: pl.semaphore_signal(
            barrier, inc=1, device_id={"strip": peer}, device_id_type=MESH
        )
    )
    inner = jnp.logical_and(has_lo, has_hi)

    @pl.when(inner)
    def _():
        pl.semaphore_wait(barrier, 2)

    @pl.when(jnp.logical_not(inner))
    def _():
        pl.semaphore_wait(barrier, 1)

    def halo(side, peer, k):
        at = pl.ds(pl.multiple_of(k * WIDE, WIDE), WIDE)
        return pltpu.make_async_remote_copy(
            src_ref=noise_hbm.at[:, :, at],
            dst_ref=(halo_hi, halo_lo)[side].at[:, :, at],
            send_sem=halo_send.at[side, k],
            recv_sem=halo_recv.at[1 - side, k],
            device_id={"strip": peer},
            device_id_type=MESH,
        )

    def halo_in(side, peer, k):
        at = pl.ds(pl.multiple_of(k * WIDE, WIDE), WIDE)
        target = (halo_lo, halo_hi)[side].at[:, :, at]
        pltpu.make_async_remote_copy(
            src_ref=target,
            dst_ref=target,
            send_sem=halo_send.at[side, k],
            recv_sem=halo_recv.at[side, k],
            device_id={"strip": peer},
            device_id_type=MESH,
        ).wait_recv()

    for k in range(chunks):
        each_side(lambda side, peer, k=k: halo(side, peer, k).start())

    @pl.when(jnp.logical_not(has_lo))
    def _():
        halo_lo[...] = jnp.zeros_like(halo_lo)

    @pl.when(jnp.logical_not(has_hi))
    def _():
        halo_hi[...] = jnp.zeros_like(halo_hi)

    smooth_hi[...] = jnp.zeros_like(smooth_hi)
    smooth_lo[...] = jnp.zeros_like(smooth_lo)
    part[...] = jnp.zeros_like(part)

    def row_block(b, carry):
        shape = (16, 3 * seasons * rows)
        out = lax.broadcasted_iota(jnp.int32, shape, 0) + b * 16
        src = lax.broadcasted_iota(jnp.int32, shape, 1)
        r, s = out // seasons, out % seasons
        block, s2, i = src // (seasons * rows), (src // rows) % seasons, src % rows
        tap = jnp.where(s == s2, (block - 1) * rows + i - r + reach, -1)
        band = jnp.zeros(shape, F32)
        for t in range(taps):
            band = jnp.where(tap == t, kern_row[t], band)
        at = pl.ds(pl.multiple_of(b * 16, 16), 16)
        row_hi[at, :], row_lo[at, :] = split(band)
        return carry

    lax.fori_loop(0, seasons * rows // 16, row_block, 0)

    def col_block(b, carry):
        shape = (16, WIDE)
        src = lax.broadcasted_iota(jnp.int32, shape, 0) + b * 16 - 128
        tap = src - lax.broadcasted_iota(jnp.int32, shape, 1) + reach
        band = jnp.zeros(shape, F32)
        for t in range(taps):
            band = jnp.where(tap == t, kern_col[t], band)
        at = pl.ds(pl.multiple_of(b * 16, 16), 16)
        col_hi[at, :], col_lo[at, :] = split(band)
        return carry

    lax.fori_loop(0, (WIDE + 256) // 16, col_block, 0)

    get_unit.wait()

    def mark(t, carry):
        k, r = t // rows, t % rows
        at = pl.ds(pl.multiple_of(k * WIDE, WIDE), WIDE)
        to = pl.ds(pl.multiple_of(t * WIDE, WIDE), WIDE)
        local = unit[pl.ds(r, 1), at] - (me - 1) * UNIT_DEV
        local = jnp.broadcast_to(local, (16, WIDE)).astype(F32)
        count = lax.broadcasted_iota(jnp.int32, (16, WIDE), 0).astype(F32)
        for b in range(3):
            mine = local - b * UNIT_DEV - count
            mine = mine.astype(BF16)
            for j in range(SPAN // 16):
                hit = jnp.where(mine == BF16(16 * j), BF16(1), BF16(0))
                onehot[b * SPAN + 16 * j : b * SPAN + 16 * j + 16, to] = hit
        return carry

    lax.fori_loop(0, rows * chunks, mark, 0)

    get_area.wait()
    get_mask.wait()
    get_base.wait()

    def weigh(c, carry):
        at = pl.ds(pl.multiple_of(c * rows, rows), rows)
        weight = mask[at, :].astype(F32) * area[...]
        weight = weight.astype(BF16).astype(F32)
        for q in range(cols // 128):
            wts[q, at, :] = weight[:, q * 128 : q * 128 + 128]
        wins[at, :] = weight * ins[c]
        wbase[at, :] = weight * base[at, :]
        return carry

    lax.fori_loop(0, crops, weigh, 0)
    get_noise.wait()

    def step(k, carry):
        @pl.when(k < chunks)
        def _():
            each_side(lambda side, peer: halo_in(side, peer, k))

            at = pl.ds(pl.multiple_of(k * WIDE, WIDE), WIDE)
            total = jnp.zeros((seasons * rows, WIDE), F32)
            for b, source in enumerate((halo_lo, noise, halo_hi)):
                high, low = split(source[:, :, at].reshape(seasons * rows, WIDE))
                lanes = slice(b * seasons * rows, (b + 1) * seasons * rows)
                total += dot(row_hi[:, lanes], high)
                total += dot(row_hi[:, lanes], low)
                total += dot(row_lo[:, lanes], high)
            to = pl.ds(pl.multiple_of(128 + k * WIDE, 128), WIDE)
            smooth_hi[:, to], smooth_lo[:, to] = split(total)

        @pl.when(k >= 1)
        def _():
            start = (k - 1) * WIDE
            at = pl.ds(pl.multiple_of(start, WIDE), WIDE + 256)
            high, low = smooth_hi[:, at], smooth_lo[:, at]
            field[...] = dot(high, col_hi[...]) + dot(low, col_hi[...]) + dot(high, col_lo[...])
            cols_at = pl.ds(pl.multiple_of(start, WIDE), WIDE)

            def fill(r, carry):
                f = field[pl.ds(pl.multiple_of(r * seasons, seasons), seasons), :] * LOG2E
                to = pl.ds(pl.multiple_of(r * WIDE, WIDE), WIDE)
                for c in range(0, crops, 2):
                    pair = [
                        wbase[pl.ds(d * rows + r, 1), cols_at] * jnp.exp2(f * sens[d])
                        for d in (c, c + 1)
                    ]
                    pair = jnp.concatenate(pair, axis=0).astype(BF16)
                    value[c * seasons : (c + 2) * seasons, to] = pair
                own = [
                    wts[(k - 1) * (WIDE // 128) + q, pl.ds(r, crops, stride=rows), :]
                    for q in range(WIDE // 128)
                ]
                value[many : many + crops, to] = jnp.concatenate(own, axis=1).astype(BF16)
                return carry

            lax.fori_loop(0, rows, fill, 0)
            cells_at = pl.ds(pl.multiple_of((k - 1) * cells, cells), cells)
            part[:, : many + crops] += lax.dot_general(
                onehot[:, cells_at],
                value[...],
                (((1,), (1,)), ((), ())),
                preferred_element_type=F32,
            )

        return carry

    lax.fori_loop(0, chunks + 1, step, 0)

    def exchange(source_of, buffers, send, recv):
        def copy(side, peer):
            return pltpu.make_async_remote_copy(
                src_ref=source_of(side),
                dst_ref=buffers[1 - side],
                send_sem=send.at[side],
                recv_sem=recv.at[1 - side],
                device_id={"strip": peer},
                device_id_type=MESH,
            )

        def arrive(side, peer):
            pltpu.make_async_remote_copy(
                src_ref=buffers[side],
                dst_ref=buffers[side],
                send_sem=send.at[side],
                recv_sem=recv.at[side],
                device_id={"strip": peer},
                device_id_type=MESH,
            ).wait_recv()

        each_side(lambda side, peer: copy(side, peer).start())

        @pl.when(jnp.logical_not(has_lo))
        def _():
            buffers[0][...] = jnp.zeros_like(buffers[0])

        @pl.when(jnp.logical_not(has_hi))
        def _():
            buffers[1][...] = jnp.zeros_like(buffers[1])

        each_side(arrive)
        return lambda: each_side(lambda side, peer: copy(side, peer).wait_send())

    part_done = exchange(
        lambda side: part.at[pl.ds(2 * side * SPAN, SPAN)], (from_lo, from_hi), part_send, part_recv
    )
    total = part[SPAN : 2 * SPAN, :] + from_lo[...] + from_hi[...]
    lane_crop = lax.broadcasted_iota(jnp.int32, (128, many), 1) // seasons
    spread = (lane_crop == lax.broadcasted_iota(jnp.int32, (128, many), 0)).astype(BF16)
    first, rest = split(total[:, many:])
    first_area = dot(first, spread)
    rest1, rest2 = split(total[:, many:] - first.astype(F32))
    denom = jnp.maximum(first_area + dot(rest1, spread) + dot(rest2, spread), 1.0)
    yields = total[:, :many] / denom
    guard = jnp.zeros((1, many), F32)
    for c in range(crops):
        guard = jnp.where(lane_crop[:1] == c, guar[c], guard)
    lack = jnp.maximum(guard - yields, 0.0) / guard
    real = lax.broadcasted_iota(jnp.int32, lack.shape, 0) < UNIT_DEV
    short[...] = jnp.where(real, lack, 0.0).astype(BF16)
    short_done = exchange(lambda side: short, (short_lo, short_hi), short_send, short_recv)

    turned[...] = jnp.concatenate([yields, jnp.zeros((128 - SPAN, many), F32)], axis=0).T
    for s in range(seasons):
        yield_out[s] = turned[pl.ds(s, crops, stride=seasons), :UNIT_DEV]

    for b, source in enumerate((short_lo, short, short_hi)):
        window[b * SPAN : (b + 1) * SPAN, :] = source[...].astype(F32)
    facing = window[...].T.astype(BF16)

    def pays(t, carry):
        k, r = t // rows, t % rows
        at = pl.ds(pl.multiple_of(k * WIDE, WIDE), WIDE)
        cells_at = pl.ds(pl.multiple_of(t * WIDE, WIDE), WIDE)
        lacking = dot(facing, onehot[:, cells_at])
        total = jnp.zeros((seasons, WIDE), F32)
        for c in range(crops):
            total += wins[pl.ds(c * rows + r, 1), at] * lacking[c * seasons : (c + 1) * seasons]
        to = pl.ds(pl.multiple_of(r * seasons, seasons), seasons)
        for q in range(WIDE // 128):
            pay[k * (WIDE // 128) + q, to, :] = total[:, q * 128 : q * 128 + 128]
        return carry

    lax.fori_loop(0, rows * chunks, pays, 0)

    for s in range(seasons):
        for q in range(cols // 128):
            out = pay[q, pl.ds(s, rows, stride=seasons), :]
            pay_out[s, :, q * 128 : q * 128 + 128] = out

    for k in range(chunks):
        each_side(lambda side, peer, k=k: halo(side, peer, k).wait_send())
    part_done()
    short_done()


def on_device(
    noise,
    kern_row,
    kern_col,
    base_yield,
    sensitivity,
    crop_mask,
    cell_area,
    cell_unit,
    guarantee,
    insured,
):
    seasons, rows, cols = noise.shape
    crops = base_yield.shape[0]
    many = seasons * crops
    n = lax.axis_size("strip")
    chunks = cols // WIDE
    hbm = pl.BlockSpec(memory_space=pl.ANY)
    smem = pl.BlockSpec(memory_space=pltpu.SMEM)
    vmem = pl.BlockSpec(memory_space=pltpu.VMEM)
    flat = (crops * rows, cols)
    return pl.pallas_call(
        functools.partial(kernel, n),
        out_shape=(
            jax.ShapeDtypeStruct((seasons, rows, cols), F32),
            jax.ShapeDtypeStruct((seasons, crops, UNIT_DEV), F32),
        ),
        in_specs=[hbm, smem, smem, hbm, smem, hbm, hbm, hbm, smem, smem],
        out_specs=(vmem, vmem),
        scratch_shapes=[
            pltpu.VMEM(noise.shape, F32),
            pltpu.VMEM(flat, F32),
            pltpu.VMEM(flat, jnp.int32),
            pltpu.VMEM((rows, cols), F32),
            pltpu.VMEM((rows, cols), jnp.int32),
            pltpu.VMEM(noise.shape, F32),
            pltpu.VMEM(noise.shape, F32),
            pltpu.VMEM((seasons * rows, 3 * seasons * rows), BF16),
            pltpu.VMEM((seasons * rows, 3 * seasons * rows), BF16),
            pltpu.VMEM((WIDE + 256, WIDE), BF16),
            pltpu.VMEM((WIDE + 256, WIDE), BF16),
            pltpu.VMEM((seasons * rows, cols + 256), BF16),
            pltpu.VMEM((seasons * rows, cols + 256), BF16),
            pltpu.VMEM((seasons * rows, WIDE), F32),
            pltpu.VMEM((3 * SPAN, rows * cols), BF16),
            pltpu.VMEM(flat, F32),
            pltpu.VMEM(flat, F32),
            pltpu.VMEM((cols // 128, crops * rows, 128), F32),
            pltpu.VMEM((many + crops, rows * WIDE), BF16),
            pltpu.VMEM((3 * SPAN, many + 128), F32),
            pltpu.VMEM((SPAN, many + 128), F32),
            pltpu.VMEM((SPAN, many + 128), F32),
            pltpu.VMEM((SPAN, many), BF16),
            pltpu.VMEM((SPAN, many), BF16),
            pltpu.VMEM((SPAN, many), BF16),
            pltpu.VMEM((many, 128), F32),
            pltpu.VMEM((3 * SPAN, many), F32),
            pltpu.VMEM((cols // 128, seasons * rows, 128), F32),
            pltpu.SemaphoreType.DMA((5,)),
            pltpu.SemaphoreType.DMA((2, chunks)),
            pltpu.SemaphoreType.DMA((2, chunks)),
            pltpu.SemaphoreType.DMA((2,)),
            pltpu.SemaphoreType.DMA((2,)),
            pltpu.SemaphoreType.DMA((2,)),
            pltpu.SemaphoreType.DMA((2,)),
        ],
        compiler_params=pltpu.CompilerParams(
            collective_id=0, has_side_effects=True, vmem_limit_bytes=56 * 2**20
        ),
    )(
        noise,
        kern_row,
        kern_col,
        base_yield.reshape(flat),
        sensitivity,
        crop_mask.reshape(flat),
        cell_area,
        cell_unit,
        guarantee,
        insured,
    )


def solution(mesh):
    in_specs = (
        P("season", "strip", None),
        P(),
        P(),
        P(None, "strip", None),
        P(),
        P(None, "strip", None),
        P("strip", None),
        P("strip", None),
        P(),
        P(),
    )
    out_specs = (P("season", "strip", None), P("season", None, "strip"))
    return jax.shard_map(
        on_device, mesh=mesh, in_specs=in_specs, out_specs=out_specs, check_vma=False
    )
```

```python
import functools

import jax
import jax.numpy as jnp
from jax import lax
from jax.experimental import pallas as pl
from jax.experimental.pallas import tpu as pltpu
from jax.sharding import PartitionSpec as P

UNIT_DEV = 102
SPAN = 104
SHORT = 112
SLOTS = 320
GROUP = 4
WIDE = 256
LOG2E = 1.4426950408889634
MESH = pl.DeviceIdType.MESH
F32 = jnp.float32
BF16 = jnp.bfloat16


def dot(a, b):
    return jnp.dot(a, b, preferred_element_type=F32)


def split(x):
    high = x.astype(BF16)
    return high, (x - high.astype(F32)).astype(BF16)


def kernel(
    n,
    noise_hbm,
    kern_row,
    kern_col,
    base_hbm,
    sens,
    mask_hbm,
    area_hbm,
    unit_hbm,
    guar,
    ins,
    pay_out,
    yield_out,
    noise,
    base,
    mask,
    area,
    unit,
    halo_lo,
    halo_hi,
    row_band,
    col_band,
    smooth_hi,
    smooth_lo,
    field,
    onehot,
    wins,
    wbase,
    wts,
    value_a,
    value_b,
    part,
    from_lo,
    from_hi,
    short,
    short_lo,
    short_hi,
    window,
    local_sem,
    halo_send,
    halo_recv,
    part_send,
    part_recv,
    short_send,
    short_recv,
):
    seasons, rows, cols = noise.shape
    crops = base.shape[0] // rows
    taps = kern_row.shape[0]
    reach = (taps - 1) // 2
    many = seasons * crops
    chunks = cols // WIDE
    me = lax.axis_index("strip")
    has_lo, has_hi = me > 0, me < n - 1

    def copies(source, target, sem):
        copy = pltpu.make_async_copy(source, target, local_sem.at[sem])
        copy.start()
        return copy

    get_unit = copies(unit_hbm, unit, 0)
    get_area = copies(area_hbm, area, 1)
    get_mask = copies(mask_hbm, mask, 2)
    get_base = copies(base_hbm, base, 3)
    get_noise = copies(noise_hbm, noise, 4)

    barrier = pltpu.get_barrier_semaphore()

    def each_side(body):
        @pl.when(has_lo)
        def _():
            body(0, me - 1)

        @pl.when(has_hi)
        def _():
            body(1, me + 1)

    each_side(
        lambda side, peer: pl.semaphore_signal(
            barrier, inc=1, device_id={"strip": peer}, device_id_type=MESH
        )
    )
    inner = jnp.logical_and(has_lo, has_hi)

    @pl.when(inner)
    def _():
        pl.semaphore_wait(barrier, 2)

    @pl.when(jnp.logical_not(inner))
    def _():
        pl.semaphore_wait(barrier, 1)

    def halo(side, peer, k):
        at = pl.ds(pl.multiple_of(k * WIDE, WIDE), WIDE)
        return pltpu.make_async_remote_copy(
            src_ref=noise_hbm.at[:, :, at],
            dst_ref=(halo_hi, halo_lo)[side].at[:, :, at],
            send_sem=halo_send.at[side, k],
            recv_sem=halo_recv.at[1 - side, k],
            device_id={"strip": peer},
            device_id_type=MESH,
        )

    def halo_in(side, peer, k):
        at = pl.ds(pl.multiple_of(k * WIDE, WIDE), WIDE)
        target = (halo_lo, halo_hi)[side].at[:, :, at]
        pltpu.make_async_remote_copy(
            src_ref=target,
            dst_ref=target,
            send_sem=halo_send.at[side, k],
            recv_sem=halo_recv.at[side, k],
            device_id={"strip": peer},
            device_id_type=MESH,
        ).wait_recv()

    for k in range(chunks):
        each_side(lambda side, peer, k=k: halo(side, peer, k).start())

    @pl.when(jnp.logical_not(has_lo))
    def _():
        halo_lo[...] = jnp.zeros_like(halo_lo)

    @pl.when(jnp.logical_not(has_hi))
    def _():
        halo_hi[...] = jnp.zeros_like(halo_hi)

    smooth_hi[...] = jnp.zeros_like(smooth_hi)
    smooth_lo[...] = jnp.zeros_like(smooth_lo)
    part[...] = jnp.zeros_like(part)

    def row_block(b, carry):
        shape = (16, 3 * seasons * rows)
        out = lax.broadcasted_iota(jnp.int32, shape, 0) + b * 16
        src = lax.broadcasted_iota(jnp.int32, shape, 1)
        r, s = out // seasons, out % seasons
        block, s2, i = src // (seasons * rows), (src // rows) % seasons, src % rows
        tap = jnp.where(s == s2, (block - 1) * rows + i - r + reach, -1)
        band = jnp.zeros(shape, F32)
        for t in range(taps):
            band = jnp.where(tap == t, kern_row[t], band)
        at = pl.ds(pl.multiple_of(b * 16, 16), 16)
        high, low = split(band)
        row_band[at, :] = jnp.concatenate([high, high, low], axis=1)
        return carry

    lax.fori_loop(0, seasons * rows // 16, row_block, 0)

    def col_block(j, carry):
        shape = (16, WIDE)
        src = lax.broadcasted_iota(jnp.int32, shape, 0) + j * 16 - 128
        tap = src - lax.broadcasted_iota(jnp.int32, shape, 1) + reach
        band = jnp.zeros(shape, F32)
        for t in range(taps):
            band = jnp.where(tap == t, kern_col[t], band)
        high, low = split(band)
        for b, piece in enumerate((high, high, low)):
            to = pl.ds(pl.multiple_of(b * (WIDE + 256) + j * 16, 16), 16)
            col_band[to, :] = piece
        return carry

    lax.fori_loop(0, (WIDE + 256) // 16, col_block, 0)

    get_unit.wait()

    def mark(t, carry):
        k, r = t // rows, t % rows
        at = pl.ds(pl.multiple_of(k * WIDE, WIDE), WIDE)
        to = pl.ds(pl.multiple_of(t * WIDE, WIDE), WIDE)
        local = unit[pl.ds(r, 1), at] - (me - 1) * UNIT_DEV
        past = jnp.where(local >= UNIT_DEV, 1, 0) + jnp.where(local >= 2 * UNIT_DEV, 1, 0)
        slot = local + past * (SPAN - UNIT_DEV) - SLOTS // 2
        slot = jnp.broadcast_to(slot, (16, WIDE))
        slot = (slot - lax.broadcasted_iota(jnp.int32, (16, WIDE), 0)).astype(F32).astype(BF16)
        for j in range(SLOTS // 16):
            hit = jnp.where(slot == BF16(16 * j - SLOTS // 2), BF16(1), BF16(0))
            onehot[16 * j : 16 * j + 16, to] = hit
        return carry

    lax.fori_loop(0, rows * chunks, mark, 0)

    get_area.wait()
    get_mask.wait()
    get_base.wait()

    def weigh(c, carry):
        at = pl.ds(pl.multiple_of(c * rows, rows), rows)
        weight = mask[at, :].astype(F32) * area[...]
        weight = weight.astype(BF16).astype(F32)
        for q in range(cols // 128):
            wts[q, at, :] = weight[:, q * 128 : q * 128 + 128]
        wins[at, :] = weight * ins[c]
        wbase[at, :] = weight * base[at, :]
        return carry

    lax.fori_loop(0, crops, weigh, 0)
    get_noise.wait()

    value_b[...] = jnp.zeros_like(value_b)

    def add(value, index):
        at = pl.ds(pl.multiple_of(index * GROUP * WIDE, GROUP * WIDE), GROUP * WIDE)
        part[:, : many + crops] += lax.dot_general(
            onehot[:, at],
            value[...],
            (((1,), (1,)), ((), ())),
            preferred_element_type=F32,
        )

    def step(k, carry):
        @pl.when(k < chunks)
        def _():
            each_side(lambda side, peer: halo_in(side, peer, k))

            at = pl.ds(pl.multiple_of(k * WIDE, WIDE), WIDE)
            parts = [
                split(source[:, :, at].reshape(seasons * rows, WIDE))
                for source in (halo_lo, noise, halo_hi)
            ]
            highs, lows = [p[0] for p in parts], [p[1] for p in parts]
            total = dot(row_band[...], jnp.concatenate(highs + lows + highs, axis=0))
            to = pl.ds(pl.multiple_of(128 + k * WIDE, 128), WIDE)
            smooth_hi[:, to], smooth_lo[:, to] = split(total)

        @pl.when(k >= 1)
        def _():
            start = (k - 1) * WIDE
            at = pl.ds(pl.multiple_of(start, WIDE), WIDE + 256)
            high, low = smooth_hi[:, at], smooth_lo[:, at]
            field[...] = dot(jnp.concatenate([high, low, high], axis=1), col_band[...]) * LOG2E
            cols_at = pl.ds(pl.multiple_of(start, WIDE), WIDE)

            def fill(value, r, to):
                f = field[pl.ds(pl.multiple_of(r * seasons, seasons), seasons), :]
                for c in range(0, crops, 2):
                    pair = [
                        wbase[pl.ds(d * rows + r, 1), cols_at] * jnp.exp2(f * sens[d])
                        for d in (c, c + 1)
                    ]
                    pair = jnp.concatenate(pair, axis=0).astype(BF16)
                    value[c * seasons : (c + 2) * seasons, to] = pair
                own = [
                    wts[(k - 1) * (WIDE // 128) + q, pl.ds(r, crops, stride=rows), :]
                    for q in range(WIDE // 128)
                ]
                value[many : many + crops, to] = jnp.concatenate(own, axis=1).astype(BF16)

            def group(i, carry):
                for half, (before, now) in enumerate(((value_b, value_a), (value_a, value_b))):
                    first = 2 * i + half
                    add(before, jnp.maximum((k - 1) * (rows // GROUP) + first - 1, 0))
                    for j in range(GROUP):
                        fill(now, first * GROUP + j, slice(j * WIDE, j * WIDE + WIDE))
                return carry

            lax.fori_loop(0, rows // (2 * GROUP), group, 0)

        return carry

    lax.fori_loop(0, chunks + 1, step, 0)
    add(value_b, chunks * (rows // GROUP) - 1)

    def exchange(source_of, buffers, send, recv):
        def copy(side, peer):
            return pltpu.make_async_remote_copy(
                src_ref=source_of(side),
                dst_ref=buffers[1 - side],
                send_sem=send.at[side],
                recv_sem=recv.at[1 - side],
                device_id={"strip": peer},
                device_id_type=MESH,
            )

        def arrive(side, peer):
            pltpu.make_async_remote_copy(
                src_ref=buffers[side],
                dst_ref=buffers[side],
                send_sem=send.at[side],
                recv_sem=recv.at[side],
                device_id={"strip": peer},
                device_id_type=MESH,
            ).wait_recv()

        each_side(lambda side, peer: copy(side, peer).start())

        @pl.when(jnp.logical_not(has_lo))
        def _():
            buffers[0][...] = jnp.zeros_like(buffers[0])

        @pl.when(jnp.logical_not(has_hi))
        def _():
            buffers[1][...] = jnp.zeros_like(buffers[1])

        each_side(arrive)
        return lambda: each_side(lambda side, peer: copy(side, peer).wait_send())

    part_done = exchange(
        lambda side: part.at[pl.ds(2 * side * SPAN, SPAN)], (from_lo, from_hi), part_send, part_recv
    )
    total = part[SPAN : 2 * SPAN, :] + from_lo[...] + from_hi[...]
    lane_crop = lax.broadcasted_iota(jnp.int32, (128, many), 1) // seasons
    spread = (lane_crop == lax.broadcasted_iota(jnp.int32, (128, many), 0)).astype(BF16)
    first, rest = split(total[:, many:])
    first_area = dot(first, spread)
    rest1, rest2 = split(total[:, many:] - first.astype(F32))
    denom = jnp.maximum(first_area + dot(rest1, spread) + dot(rest2, spread), 1.0)
    yields = total[:, :many] / denom
    guard = jnp.zeros((1, many), F32)
    for c in range(crops):
        guard = jnp.where(lane_crop[:1] == c, guar[c], guard)
    lack = jnp.maximum(guard - yields, 0.0) / guard
    real = lax.broadcasted_iota(jnp.int32, lack.shape, 0) < UNIT_DEV
    lack = jnp.where(real, lack, 0.0)
    none = jnp.zeros((SHORT - SPAN, many), F32)
    short[...] = jnp.concatenate([lack, none], axis=0).astype(BF16)
    short_done = exchange(lambda side: short, (short_lo, short_hi), short_send, short_recv)

    yield_out[...] = jnp.concatenate([yields, jnp.zeros((128 - SPAN, many), F32)], axis=0).T

    for b, source in enumerate((short_lo, short, short_hi)):
        window[b * SPAN : (b + 1) * SPAN, :] = source[...].astype(F32)[:SPAN]
    window[3 * SPAN :, :] = jnp.zeros((SLOTS - 3 * SPAN, many), F32)
    facing = window[...].T.astype(BF16)

    def pays(t, carry):
        k, r = t // rows, t % rows
        at = pl.ds(pl.multiple_of(k * WIDE, WIDE), WIDE)
        cells_at = pl.ds(pl.multiple_of(t * WIDE, WIDE), WIDE)
        lacking = dot(facing, onehot[:, cells_at])
        total = jnp.zeros((seasons, WIDE), F32)
        for c in range(crops):
            total += wins[pl.ds(c * rows + r, 1), at] * lacking[c * seasons : (c + 1) * seasons]
        to = pl.ds(pl.multiple_of(r * seasons, seasons), seasons)
        for q in range(WIDE // 128):
            pay_out[k * (WIDE // 128) + q, to, :] = total[:, q * 128 : q * 128 + 128]
        return carry

    lax.fori_loop(0, rows * chunks, pays, 0, unroll=8)

    for k in range(chunks):
        each_side(lambda side, peer, k=k: halo(side, peer, k).wait_send())
    part_done()
    short_done()


def unravel(pay, yields, pay_out, yield_out):
    seasons, rows, cols = pay_out.shape
    crops = yield_out.shape[1]
    for s in range(seasons):
        yield_out[s] = yields[pl.ds(s, crops, stride=seasons), :][:, :UNIT_DEV]
        for q in range(cols // 128):
            out = pay[q, pl.ds(s, rows, stride=seasons), :]
            pay_out[s, :, q * 128 : q * 128 + 128] = out


def on_device(
    noise,
    kern_row,
    kern_col,
    base_yield,
    sensitivity,
    crop_mask,
    cell_area,
    cell_unit,
    guarantee,
    insured,
):
    seasons, rows, cols = noise.shape
    crops = base_yield.shape[0]
    many = seasons * crops
    n = lax.axis_size("strip")
    chunks = cols // WIDE
    hbm = pl.BlockSpec(memory_space=pl.ANY)
    smem = pl.BlockSpec(memory_space=pltpu.SMEM)
    vmem = pl.BlockSpec(memory_space=pltpu.VMEM)
    flat = (crops * rows, cols)
    pay, yields = pl.pallas_call(
        functools.partial(kernel, n),
        out_shape=(
            jax.ShapeDtypeStruct((cols // 128, seasons * rows, 128), F32),
            jax.ShapeDtypeStruct((many, 128), F32),
        ),
        in_specs=[hbm, smem, smem, hbm, smem, hbm, hbm, hbm, smem, smem],
        out_specs=(vmem, vmem),
        scratch_shapes=[
            pltpu.VMEM(noise.shape, F32),
            pltpu.VMEM(flat, F32),
            pltpu.VMEM(flat, jnp.int32),
            pltpu.VMEM((rows, cols), F32),
            pltpu.VMEM((rows, cols), jnp.int32),
            pltpu.VMEM(noise.shape, F32),
            pltpu.VMEM(noise.shape, F32),
            pltpu.VMEM((seasons * rows, 9 * seasons * rows), BF16),
            pltpu.VMEM((3 * (WIDE + 256), WIDE), BF16),
            pltpu.VMEM((seasons * rows, cols + 256), BF16),
            pltpu.VMEM((seasons * rows, cols + 256), BF16),
            pltpu.VMEM((seasons * rows, WIDE), F32),
            pltpu.VMEM((SLOTS, rows * cols), BF16),
            pltpu.VMEM(flat, F32),
            pltpu.VMEM(flat, F32),
            pltpu.VMEM((cols // 128, crops * rows, 128), F32),
            pltpu.VMEM((many + crops, GROUP * WIDE), BF16),
            pltpu.VMEM((many + crops, GROUP * WIDE), BF16),
            pltpu.VMEM((SLOTS, many + 128), F32),
            pltpu.VMEM((SPAN, many + 128), F32),
            pltpu.VMEM((SPAN, many + 128), F32),
            pltpu.VMEM((SHORT, many), BF16),
            pltpu.VMEM((SHORT, many), BF16),
            pltpu.VMEM((SHORT, many), BF16),
            pltpu.VMEM((SLOTS, many), F32),
            pltpu.SemaphoreType.DMA((5,)),
            pltpu.SemaphoreType.DMA((2, chunks)),
            pltpu.SemaphoreType.DMA((2, chunks)),
            pltpu.SemaphoreType.DMA((2,)),
            pltpu.SemaphoreType.DMA((2,)),
            pltpu.SemaphoreType.DMA((2,)),
            pltpu.SemaphoreType.DMA((2,)),
        ],
        compiler_params=pltpu.CompilerParams(
            collective_id=0, has_side_effects=True, vmem_limit_bytes=56 * 2**20
        ),
    )(
        noise,
        kern_row,
        kern_col,
        base_yield.reshape(flat),
        sensitivity,
        crop_mask.reshape(flat),
        cell_area,
        cell_unit,
        guarantee,
        insured,
    )
    return pl.pallas_call(
        unravel,
        out_shape=(
            jax.ShapeDtypeStruct((seasons, rows, cols), F32),
            jax.ShapeDtypeStruct((seasons, crops, UNIT_DEV), F32),
        ),
        in_specs=[vmem, vmem],
        out_specs=(vmem, vmem),
    )(pay, yields)


def solution(mesh):
    in_specs = (
        P("season", "strip", None),
        P(),
        P(),
        P(None, "strip", None),
        P(),
        P(None, "strip", None),
        P("strip", None),
        P("strip", None),
        P(),
        P(),
    )
    out_specs = (P("season", "strip", None), P("season", None, "strip"))
    return jax.shard_map(
        on_device, mesh=mesh, in_specs=in_specs, out_specs=out_specs, check_vma=False
    )
```

```python
import functools

import jax
import jax.numpy as jnp
from jax import lax
from jax.experimental import pallas as pl
from jax.experimental.pallas import tpu as pltpu
from jax.sharding import PartitionSpec as P

UNIT_DEV = 102
SPAN = 104
SHORT = 112
SLOTS = 320
GROUP = 8
WIDE = 256
LOG2E = 1.4426950408889634
MESH = pl.DeviceIdType.MESH
F32 = jnp.float32
BF16 = jnp.bfloat16


def dot(a, b):
    return jnp.dot(a, b, preferred_element_type=F32)


def split(x):
    high = x.astype(BF16)
    return high, (x - high.astype(F32)).astype(BF16)


def kernel(
    n,
    noise_hbm,
    kern_row,
    kern_col,
    base_hbm,
    sens,
    mask_hbm,
    area_hbm,
    unit_hbm,
    guar,
    ins,
    pay_out,
    yield_out,
    noise,
    base,
    mask,
    area,
    unit,
    halo_lo,
    halo_hi,
    row_band,
    col_band,
    smooth_hi,
    smooth_lo,
    field,
    onehot,
    wins,
    wbase,
    wts,
    value_a,
    value_b,
    part,
    from_lo,
    from_hi,
    short,
    short_lo,
    short_hi,
    window,
    local_sem,
    halo_send,
    halo_recv,
    part_send,
    part_recv,
    short_send,
    short_recv,
):
    seasons, rows, cols = noise.shape
    crops = base.shape[0] // rows
    taps = kern_row.shape[0]
    reach = (taps - 1) // 2
    many = seasons * crops
    chunks = cols // WIDE
    me = lax.axis_index("strip")
    has_lo, has_hi = me > 0, me < n - 1

    def copies(source, target, sem):
        copy = pltpu.make_async_copy(source, target, local_sem.at[sem])
        copy.start()
        return copy

    get_unit = copies(unit_hbm, unit, 0)
    get_area = copies(area_hbm, area, 1)
    get_mask = copies(mask_hbm, mask, 2)
    get_base = copies(base_hbm, base, 3)
    get_noise = copies(noise_hbm, noise, 4)

    barrier = pltpu.get_barrier_semaphore()

    def each_side(body):
        @pl.when(has_lo)
        def _():
            body(0, me - 1)

        @pl.when(has_hi)
        def _():
            body(1, me + 1)

    each_side(
        lambda side, peer: pl.semaphore_signal(
            barrier, inc=1, device_id={"strip": peer}, device_id_type=MESH
        )
    )
    inner = jnp.logical_and(has_lo, has_hi)

    @pl.when(inner)
    def _():
        pl.semaphore_wait(barrier, 2)

    @pl.when(jnp.logical_not(inner))
    def _():
        pl.semaphore_wait(barrier, 1)

    def halo(side, peer, k):
        at = pl.ds(pl.multiple_of(k * WIDE, WIDE), WIDE)
        return pltpu.make_async_remote_copy(
            src_ref=noise_hbm.at[:, :, at],
            dst_ref=(halo_hi, halo_lo)[side].at[:, :, at],
            send_sem=halo_send.at[side, k],
            recv_sem=halo_recv.at[1 - side, k],
            device_id={"strip": peer},
            device_id_type=MESH,
        )

    def halo_in(side, peer, k):
        at = pl.ds(pl.multiple_of(k * WIDE, WIDE), WIDE)
        target = (halo_lo, halo_hi)[side].at[:, :, at]
        pltpu.make_async_remote_copy(
            src_ref=target,
            dst_ref=target,
            send_sem=halo_send.at[side, k],
            recv_sem=halo_recv.at[side, k],
            device_id={"strip": peer},
            device_id_type=MESH,
        ).wait_recv()

    for k in range(chunks):
        each_side(lambda side, peer, k=k: halo(side, peer, k).start())

    @pl.when(jnp.logical_not(has_lo))
    def _():
        halo_lo[...] = jnp.zeros_like(halo_lo)

    @pl.when(jnp.logical_not(has_hi))
    def _():
        halo_hi[...] = jnp.zeros_like(halo_hi)

    smooth_hi[...] = jnp.zeros_like(smooth_hi)
    smooth_lo[...] = jnp.zeros_like(smooth_lo)
    part[...] = jnp.zeros_like(part)

    def row_block(b, carry):
        shape = (16, 3 * seasons * rows)
        out = lax.broadcasted_iota(jnp.int32, shape, 0) + b * 16
        src = lax.broadcasted_iota(jnp.int32, shape, 1)
        r, s = out // seasons, out % seasons
        block, s2, i = src // (seasons * rows), (src // rows) % seasons, src % rows
        tap = jnp.where(s == s2, (block - 1) * rows + i - r + reach, -1)
        band = jnp.zeros(shape, F32)
        for t in range(taps):
            band = jnp.where(tap == t, kern_row[t], band)
        at = pl.ds(pl.multiple_of(b * 16, 16), 16)
        high, low = split(band)
        row_band[at, :] = jnp.concatenate([high, high, low], axis=1)
        return carry

    lax.fori_loop(0, seasons * rows // 16, row_block, 0)

    def col_block(j, carry):
        shape = (16, WIDE)
        src = lax.broadcasted_iota(jnp.int32, shape, 0) + j * 16 - 128
        tap = src - lax.broadcasted_iota(jnp.int32, shape, 1) + reach
        band = jnp.zeros(shape, F32)
        for t in range(taps):
            band = jnp.where(tap == t, kern_col[t], band)
        high, low = split(band)
        for b, piece in enumerate((high, high, low)):
            to = pl.ds(pl.multiple_of(b * (WIDE + 256) + j * 16, 16), 16)
            col_band[to, :] = piece
        return carry

    lax.fori_loop(0, (WIDE + 256) // 16, col_block, 0)

    get_unit.wait()

    def mark(t, carry):
        k, r = t // rows, t % rows
        at = pl.ds(pl.multiple_of(k * WIDE, WIDE), WIDE)
        to = pl.ds(pl.multiple_of(t * WIDE, WIDE), WIDE)
        local = unit[pl.ds(r, 1), at] - (me - 1) * UNIT_DEV
        past = jnp.where(local >= UNIT_DEV, 1, 0) + jnp.where(local >= 2 * UNIT_DEV, 1, 0)
        slot = local + past * (SPAN - UNIT_DEV) - SLOTS // 2
        slot = jnp.broadcast_to(slot, (16, WIDE))
        slot = (slot - lax.broadcasted_iota(jnp.int32, (16, WIDE), 0)).astype(F32).astype(BF16)
        for j in range(SLOTS // 16):
            hit = jnp.where(slot == BF16(16 * j - SLOTS // 2), BF16(1), BF16(0))
            onehot[16 * j : 16 * j + 16, to] = hit
        return carry

    lax.fori_loop(0, rows * chunks, mark, 0, unroll=2)

    get_area.wait()
    get_mask.wait()
    get_base.wait()

    def weigh(c, carry):
        at = pl.ds(pl.multiple_of(c * rows, rows), rows)
        weight = mask[at, :].astype(F32) * area[...]
        weight = weight.astype(BF16).astype(F32)
        for q in range(cols // 128):
            wts[q, at, :] = weight[:, q * 128 : q * 128 + 128]
        wins[at, :] = weight * ins[c]
        wbase[at, :] = weight * base[at, :]
        return carry

    lax.fori_loop(0, crops, weigh, 0)
    get_noise.wait()

    value_b[...] = jnp.zeros_like(value_b)

    def add(value, index):
        at = pl.ds(pl.multiple_of(index * GROUP * WIDE, GROUP * WIDE), GROUP * WIDE)
        part[:, : many + crops] += lax.dot_general(
            onehot[:, at],
            value[...],
            (((1,), (1,)), ((), ())),
            preferred_element_type=F32,
        )

    def smooth_rows(k):
        each_side(lambda side, peer: halo_in(side, peer, k))
        at = pl.ds(pl.multiple_of(k * WIDE, WIDE), WIDE)
        parts = [
            split(source[:, :, at].reshape(seasons * rows, WIDE))
            for source in (halo_lo, noise, halo_hi)
        ]
        highs, lows = [p[0] for p in parts], [p[1] for p in parts]
        total = dot(row_band[...], jnp.concatenate(highs + lows + highs, axis=0))
        to = pl.ds(pl.multiple_of(128 + k * WIDE, 128), WIDE)
        smooth_hi[:, to], smooth_lo[:, to] = split(total)

    def smooth_cols(k):
        at = pl.ds(pl.multiple_of(k * WIDE, WIDE), WIDE + 256)
        high, low = smooth_hi[:, at], smooth_lo[:, at]
        return dot(jnp.concatenate([high, low, high], axis=1), col_band[...]) * LOG2E

    def fill(value, k, r, to):
        cols_at = pl.ds(pl.multiple_of(k * WIDE, WIDE), WIDE)
        f = field[r * seasons : (r + 1) * seasons, :]
        for c in range(0, crops, 2):
            pair = [
                wbase[pl.ds(d * rows + r, 1), cols_at] * jnp.exp2(f * sens[d])
                for d in (c, c + 1)
            ]
            pair = jnp.concatenate(pair, axis=0).astype(BF16)
            value[c * seasons : (c + 2) * seasons, to] = pair
        own = [
            wts[k * (WIDE // 128) + q, pl.ds(r, crops, stride=rows), :]
            for q in range(WIDE // 128)
        ]
        value[many : many + crops, to] = jnp.concatenate(own, axis=1).astype(BF16)

    def consume(k):
        for first in range(rows // GROUP):
            before, now = ((value_b, value_a), (value_a, value_b))[first % 2]
            add(before, jnp.maximum(k * (rows // GROUP) + first - 1, 0))
            for j in range(GROUP):
                fill(now, k, first * GROUP + j, slice(j * WIDE, j * WIDE + WIDE))

    def step(k, carry):
        smooth_rows(k)
        following = smooth_cols(k - 1)
        consume(k - 2)
        field[...] = following
        return carry

    smooth_rows(0)
    smooth_rows(1)
    field[...] = smooth_cols(0)
    lax.fori_loop(2, chunks, step, 0)
    following = smooth_cols(chunks - 1)
    consume(chunks - 2)
    field[...] = following
    consume(chunks - 1)
    add(value_b, chunks * (rows // GROUP) - 1)

    def exchange(source_of, buffers, send, recv):
        def copy(side, peer):
            return pltpu.make_async_remote_copy(
                src_ref=source_of(side),
                dst_ref=buffers[1 - side],
                send_sem=send.at[side],
                recv_sem=recv.at[1 - side],
                device_id={"strip": peer},
                device_id_type=MESH,
            )

        def arrive(side, peer):
            pltpu.make_async_remote_copy(
                src_ref=buffers[side],
                dst_ref=buffers[side],
                send_sem=send.at[side],
                recv_sem=recv.at[side],
                device_id={"strip": peer},
                device_id_type=MESH,
            ).wait_recv()

        each_side(lambda side, peer: copy(side, peer).start())

        @pl.when(jnp.logical_not(has_lo))
        def _():
            buffers[0][...] = jnp.zeros_like(buffers[0])

        @pl.when(jnp.logical_not(has_hi))
        def _():
            buffers[1][...] = jnp.zeros_like(buffers[1])

        each_side(arrive)
        return lambda: each_side(lambda side, peer: copy(side, peer).wait_send())

    part_done = exchange(
        lambda side: part.at[pl.ds(2 * side * SPAN, SPAN)], (from_lo, from_hi), part_send, part_recv
    )
    total = part[SPAN : 2 * SPAN, :] + from_lo[...] + from_hi[...]
    lane_crop = lax.broadcasted_iota(jnp.int32, (128, many), 1) // seasons
    spread = (lane_crop == lax.broadcasted_iota(jnp.int32, (128, many), 0)).astype(BF16)
    first, rest = split(total[:, many:])
    first_area = dot(first, spread)
    rest1, rest2 = split(total[:, many:] - first.astype(F32))
    denom = jnp.maximum(first_area + dot(rest1, spread) + dot(rest2, spread), 1.0)
    yields = total[:, :many] / denom
    guard = jnp.zeros((1, many), F32)
    for c in range(crops):
        guard = jnp.where(lane_crop[:1] == c, guar[c], guard)
    lack = jnp.maximum(guard - yields, 0.0) / guard
    real = lax.broadcasted_iota(jnp.int32, lack.shape, 0) < UNIT_DEV
    lack = jnp.where(real, lack, 0.0)
    none = jnp.zeros((SHORT - SPAN, many), F32)
    short[...] = jnp.concatenate([lack, none], axis=0).astype(BF16)
    short_done = exchange(lambda side: short, (short_lo, short_hi), short_send, short_recv)

    yield_out[...] = jnp.concatenate([yields, jnp.zeros((128 - SPAN, many), F32)], axis=0).T

    for b, source in enumerate((short_lo, short, short_hi)):
        window[b * SPAN : (b + 1) * SPAN, :] = source[...].astype(F32)[:SPAN]
    window[3 * SPAN :, :] = jnp.zeros((SLOTS - 3 * SPAN, many), F32)
    facing = window[...].T.astype(BF16)

    def pays(t, carry):
        k, r = t // rows, t % rows
        at = pl.ds(pl.multiple_of(k * WIDE, WIDE), WIDE)
        cells_at = pl.ds(pl.multiple_of(t * WIDE, WIDE), WIDE)
        lacking = dot(facing, onehot[:, cells_at])
        total = jnp.zeros((seasons, WIDE), F32)
        for c in range(crops):
            total += wins[pl.ds(c * rows + r, 1), at] * lacking[c * seasons : (c + 1) * seasons]
        to = pl.ds(pl.multiple_of(r * seasons, seasons), seasons)
        for q in range(WIDE // 128):
            pay_out[k * (WIDE // 128) + q, to, :] = total[:, q * 128 : q * 128 + 128]
        return carry

    lax.fori_loop(0, rows * chunks, pays, 0, unroll=16)

    for k in range(chunks):
        each_side(lambda side, peer, k=k: halo(side, peer, k).wait_send())
    part_done()
    short_done()


def unravel(pay, yields, pay_out, yield_out):
    seasons, rows, cols = pay_out.shape
    crops = yield_out.shape[1]
    for s in range(seasons):
        yield_out[s] = yields[pl.ds(s, crops, stride=seasons), :][:, :UNIT_DEV]
        for q in range(cols // 128):
            out = pay[q, pl.ds(s, rows, stride=seasons), :]
            pay_out[s, :, q * 128 : q * 128 + 128] = out


def on_device(
    noise,
    kern_row,
    kern_col,
    base_yield,
    sensitivity,
    crop_mask,
    cell_area,
    cell_unit,
    guarantee,
    insured,
):
    seasons, rows, cols = noise.shape
    crops = base_yield.shape[0]
    many = seasons * crops
    n = lax.axis_size("strip")
    chunks = cols // WIDE
    hbm = pl.BlockSpec(memory_space=pl.ANY)
    smem = pl.BlockSpec(memory_space=pltpu.SMEM)
    vmem = pl.BlockSpec(memory_space=pltpu.VMEM)
    flat = (crops * rows, cols)
    pay, yields = pl.pallas_call(
        functools.partial(kernel, n),
        out_shape=(
            jax.ShapeDtypeStruct((cols // 128, seasons * rows, 128), F32),
            jax.ShapeDtypeStruct((many, 128), F32),
        ),
        in_specs=[hbm, smem, smem, hbm, smem, hbm, hbm, hbm, smem, smem],
        out_specs=(vmem, vmem),
        scratch_shapes=[
            pltpu.VMEM(noise.shape, F32),
            pltpu.VMEM(flat, F32),
            pltpu.VMEM(flat, jnp.int32),
            pltpu.VMEM((rows, cols), F32),
            pltpu.VMEM((rows, cols), jnp.int32),
            pltpu.VMEM(noise.shape, F32),
            pltpu.VMEM(noise.shape, F32),
            pltpu.VMEM((seasons * rows, 9 * seasons * rows), BF16),
            pltpu.VMEM((3 * (WIDE + 256), WIDE), BF16),
            pltpu.VMEM((seasons * rows, cols + 256), BF16),
            pltpu.VMEM((seasons * rows, cols + 256), BF16),
            pltpu.VMEM((seasons * rows, WIDE), F32),
            pltpu.VMEM((SLOTS, rows * cols), BF16),
            pltpu.VMEM(flat, F32),
            pltpu.VMEM(flat, F32),
            pltpu.VMEM((cols // 128, crops * rows, 128), F32),
            pltpu.VMEM((many + crops, GROUP * WIDE), BF16),
            pltpu.VMEM((many + crops, GROUP * WIDE), BF16),
            pltpu.VMEM((SLOTS, many + 128), F32),
            pltpu.VMEM((SPAN, many + 128), F32),
            pltpu.VMEM((SPAN, many + 128), F32),
            pltpu.VMEM((SHORT, many), BF16),
            pltpu.VMEM((SHORT, many), BF16),
            pltpu.VMEM((SHORT, many), BF16),
            pltpu.VMEM((SLOTS, many), F32),
            pltpu.SemaphoreType.DMA((5,)),
            pltpu.SemaphoreType.DMA((2, chunks)),
            pltpu.SemaphoreType.DMA((2, chunks)),
            pltpu.SemaphoreType.DMA((2,)),
            pltpu.SemaphoreType.DMA((2,)),
            pltpu.SemaphoreType.DMA((2,)),
            pltpu.SemaphoreType.DMA((2,)),
        ],
        compiler_params=pltpu.CompilerParams(
            collective_id=0, has_side_effects=True, vmem_limit_bytes=56 * 2**20
        ),
    )(
        noise,
        kern_row,
        kern_col,
        base_yield.reshape(flat),
        sensitivity,
        crop_mask.reshape(flat),
        cell_area,
        cell_unit,
        guarantee,
        insured,
    )
    return pl.pallas_call(
        unravel,
        out_shape=(
            jax.ShapeDtypeStruct((seasons, rows, cols), F32),
            jax.ShapeDtypeStruct((seasons, crops, UNIT_DEV), F32),
        ),
        grid=(2,),
        in_specs=[
            pl.BlockSpec((cols // 256, seasons * rows, 128), lambda i: (i, 0, 0)),
            pl.BlockSpec((many, 128), lambda i: (0, 0)),
        ],
        out_specs=(
            pl.BlockSpec((seasons, rows, cols // 2), lambda i: (0, 0, i)),
            pl.BlockSpec((seasons, crops, UNIT_DEV), lambda i: (0, 0, 0)),
        ),
    )(pay, yields)


def solution(mesh):
    in_specs = (
        P("season", "strip", None),
        P(),
        P(),
        P(None, "strip", None),
        P(),
        P(None, "strip", None),
        P("strip", None),
        P("strip", None),
        P(),
        P(),
    )
    out_specs = (P("season", "strip", None), P("season", None, "strip"))
    return jax.shard_map(
        on_device, mesh=mesh, in_specs=in_specs, out_specs=out_specs, check_vma=False
    )
```
